32 devices in a mesh: pipe: 1, expert: 32 (over z, y, x, core).
Axes of the slice: x: 2, y: 2, z: 4, core: 2. Of those that a mesh axis runs over, the one named last changes fastest.
Arguments:
- fwd_tokens: bfloat16 [1, 512, 3584], P('pipe', 'expert'), may hold values from -6 to 6
- fwd_routes: int32 [1, 512, 2], P('pipe', 'expert'), may hold values from 0 to 3, all different within a row; in each aligned block of 16 rows (0 to 15, 16 to 31, ..., all dimensions but the last counted through in order) at most 10 rows name the same one
- fwd_scores: float32 [1, 512, 2], P('pipe', 'expert'), may hold values from 0.1 to 1
- bwd_tokens: bfloat16 [1, 512, 3584], P('pipe', 'expert'), may hold values from -6 to 6
- bwd_routes: int32 [1, 512, 2], P('pipe', 'expert'), may hold values from 0 to 3, all different within a row; in each aligned block of 16 rows (0 to 15, 16 to 31, ..., all dimensions but the last counted through in order) at most 10 rows name the same one
- bwd_scores: float32 [1, 512, 2], P('pipe', 'expert'), may hold values from 0.1 to 1
- out_grad: bfloat16 [1, 512, 3584], P('pipe', 'expert'), may hold values from -6 to 6
- gate_weight: bfloat16 [1, 3584, 4096], P('pipe', None, 'expert'), may hold values from -0.09375 to 0.09375
- up_weight: bfloat16 [1, 3584, 4096], P('pipe', None, 'expert'), may hold values from -0.09375 to 0.09375
- down_weight: bfloat16 [1, 4096, 3584], P('pipe', 'expert'), may hold values from -0.1875 to 0.1875
Outputs:
- next_input: bfloat16 [1, 512, 3584], P('pipe', 'expert')
- prev_grad: bfloat16 [1, 512, 3584], P('pipe', 'expert')
The draws below stay inside these ranges and needn't reach their ends.
Inputs may be any that keep to these rules, and one draw needn't show every extreme that they name: `fwd_routes`: each row names 2 different experts. Among the 16 rows of one device in one section, no expert is named more than 10 times, a bound that some block reaches. `bwd_routes`: each row names 2 different experts. Among the 16 rows of one device in one section, no expert is named more than 10 times, a bound that some block reaches.
All inputs are finite; a program needn't handle non-finite values.
Results may differ from the reference program's by a relative error of at most 0.011.
Values may be sent and summed in bfloat16 or wider, within the bound.
A program may use at most 128 MiB of HBM per device.

```python
import math
import jax
import jax.numpy as jnp
import numpy as np

D = 3584
HIDDEN_SIZE = 1024
GROUP = 8
TOPK = 2
TOK_DEV = 16
H_DEV = 128
EXPERTS = 4
SECTIONS = 1
TOKENS = 512
CAP = 10
N_EXPERT = 32


def steps_of(key, shape, split, least, high):
    gain, own = 1.0, jax.random.fold_in(key, 6)
    for dim, blocks in split:
        draws = jnp.exp(jax.random.uniform(jax.random.fold_in(own, dim), (blocks,), jnp.float32, least / len(split), high / len(split)))
        gain = gain * jnp.repeat(draws, shape[dim] // blocks).reshape([-1 if axis == dim else 1 for axis in range(len(shape))])
    return gain


def shared_out(own_key, own, number, rows, number_of, top, most, lean):
    sequence = jax.random.permutation(own_key, number_of)
    packed, common = load_shares(number_of, rows * top, most, lean, True), load_shares(number_of, rows * top, most, lean, False)
    places = jnp.arange(number_of)

    def named(sizes, rotation):
        used = int((sizes > 0).sum())
        fixed = max(1, used // 4)
        passed = fixed + (places - fixed + rotation * (used - fixed)) % max(1, number_of - fixed)
        return jnp.zeros((number_of,), jnp.int32).at[sequence[jnp.where(places < fixed, places, passed)]].set(jnp.asarray(sizes, jnp.int32))

    sizes = jnp.where(number % 4 == 0, named(packed, number // 4), named(common, number - number // 4 - 1))
    mixed = jax.random.permutation(jax.random.fold_in(own, 3), number_of)
    source_of, taker = mixed[0:number_of // 2 * 2:2], mixed[1:number_of // 2 * 2:2]
    margin = jnp.minimum(sizes[source_of] - 1, most - sizes[taker]) // 2
    margin = jnp.where((source_of == sequence[0]) | (taker == sequence[0]) | (sizes[taker] == 0), 0, jnp.maximum(margin, 0))
    passed = jax.random.randint(jax.random.fold_in(own, 4), (number_of // 2,), 0, 1 << 20) % (margin + 1)
    sizes = sizes.at[source_of].add(-passed).at[taker].add(passed)
    items = jnp.searchsorted(jnp.cumsum(sizes), jnp.arange(rows * top), side="right").astype(jnp.int32)
    grid = items.reshape(top, rows).T
    grid = grid[jax.random.permutation(jax.random.fold_in(own, 1), rows)]
    rotation = jax.random.randint(jax.random.fold_in(own, 2), (rows, 1), 0, top)
    return jnp.take_along_axis(grid, (jnp.arange(top)[None, :] + rotation) % top, axis=1)


def load_shares(count, total, limit, lean, full):
    loads = [(1 << 20) // math.isqrt(rank ** lean) + 1 for rank in range(1, count + 1)]
    largest = limit if full else min(limit, max(-(-total // count), total * loads[0] // sum(loads)))
    least = 1 if total - largest >= count - 1 else 0
    given, spare = [largest] + [least] * (count - 1), total - largest - least * (count - 1)
    while spare > 0:
        candidates = [i for i in range(1, count) if given[i] < largest] or [i for i in range(1, count) if given[i] < limit]
        whole, remaining = sum([loads[i] for i in candidates]), spare
        for i in candidates:
            more = min(limit - given[i], max(1, remaining * loads[i] // whole), spare)
            given[i] = given[i] + more
            spare = spare - more
    return np.array(given)


def noise(stream_key, shape, scale, reach, split=(), kind=jnp.bfloat16):
    result = scale * jax.random.normal(stream_key, shape, jnp.float32)
    if split:
        result = result * steps_of(stream_key, shape, split, -0.22, 0.18)
    return jnp.clip(result, -reach, reach).astype(kind)


def setup_inputs(seed: int = 0) -> dict:
    key_list = jax.random.split(jax.random.key(seed), 11)
    fwd_tokens = noise(key_list[0], (SECTIONS, TOKENS, D), 1.0, 6.0, ((1, 32),))
    fwd_routes_keys = jax.random.split(jax.random.fold_in(key_list[1], 1), SECTIONS * TOKENS // TOK_DEV)
    fwd_routes_turns = jax.random.permutation(jax.random.fold_in(key_list[1], 3), SECTIONS * TOKENS // TOK_DEV)
    fwd_routes = jax.vmap(lambda own, number: shared_out(jax.random.fold_in(key_list[1], 2), own, number, TOK_DEV, EXPERTS, TOPK, CAP, 2))(fwd_routes_keys, fwd_routes_turns).reshape((SECTIONS, TOKENS, TOPK))
    fwd_scores = jnp.clip(jnp.exp(math.log(1.0) - 2.3025851 * jax.random.uniform(key_list[2], (SECTIONS, TOKENS, TOPK), jnp.float32) ** steps_of(key_list[2], (SECTIONS, TOKENS, TOPK), ((1, 32),), -0.2, 0.2)), 0.1, 1.0)
    bwd_tokens = noise(key_list[3], (SECTIONS, TOKENS, D), 1.0, 6.0, ((1, 32),))
    bwd_routes_keys = jax.random.split(jax.random.fold_in(key_list[4], 1), SECTIONS * TOKENS // TOK_DEV)
    bwd_routes_turns = jax.random.permutation(jax.random.fold_in(key_list[4], 3), SECTIONS * TOKENS // TOK_DEV)
    bwd_routes = jax.vmap(lambda own, number: shared_out(jax.random.fold_in(key_list[4], 2), own, number, TOK_DEV, EXPERTS, TOPK, CAP, 2))(bwd_routes_keys, bwd_routes_turns).reshape((SECTIONS, TOKENS, TOPK))
    bwd_scores = jnp.clip(jnp.exp(math.log(1.0) - 2.3025851 * jax.random.uniform(key_list[5], (SECTIONS, TOKENS, TOPK), jnp.float32) ** steps_of(key_list[5], (SECTIONS, TOKENS, TOPK), ((1, 32),), -0.2, 0.2)), 0.1, 1.0)
    out_grad = noise(key_list[6], (SECTIONS, TOKENS, D), 1.0, 6.0, ((1, 32),))
    gate_weight = noise(key_list[7], (SECTIONS, D, EXPERTS * HIDDEN_SIZE), D ** -0.5, 0.09375, ((2, 32),))
    up_weight = noise(key_list[8], (SECTIONS, D, EXPERTS * HIDDEN_SIZE), D ** -0.5, 0.09375, ((2, 32),))
    down_weight = noise(key_list[9], (SECTIONS, EXPERTS * HIDDEN_SIZE, D), HIDDEN_SIZE ** -0.5, 0.1875, ((1, 32),))
    return dict(fwd_tokens=fwd_tokens, fwd_routes=fwd_routes, fwd_scores=fwd_scores, bwd_tokens=bwd_tokens, bwd_routes=bwd_routes, bwd_scores=bwd_scores, out_grad=out_grad, gate_weight=gate_weight, up_weight=up_weight, down_weight=down_weight)


def slot_places(routes):
    blocks = routes.reshape(N_EXPERT, TOK_DEV * TOPK)
    onehot = (blocks[:, :, None] == jnp.arange(EXPERTS, dtype=jnp.int32)[None, None, :]).astype(jnp.int32)
    rank = jnp.cumsum(onehot, axis=1) - onehot
    within = jnp.sum(rank * onehot, axis=2)
    anchor = (jnp.arange(N_EXPERT, dtype=jnp.int32) * CAP)[:, None]
    return blocks.reshape(-1), (anchor + within).reshape(-1).astype(jnp.int32)


def populate_slots(rows, experts_of, places):
    width = rows.shape[-1]
    empty = jnp.zeros((EXPERTS, N_EXPERT * CAP, width), rows.dtype)
    return empty.at[experts_of, places].set(rows)


def section_pass(xf, rf, sf, xb, rb, sb, grad, wg_all, wu_all, wd_all):
    norm_f = sf / jnp.sum(sf, axis=1, keepdims=True)
    norm_b = sb / jnp.sum(sb, axis=1, keepdims=True)
    ef, pf = slot_places(rf)
    expert_batch, param_bundle = slot_places(rb)
    fbuf = populate_slots(jnp.repeat(xf, TOPK, axis=0), ef, pf)
    bbuf = populate_slots(jnp.repeat(xb, TOPK, axis=0), expert_batch, param_bundle)
    queued_rows = (norm_b.reshape(-1)[:, None] * jnp.repeat(grad, TOPK, axis=0).astype(jnp.float32)).astype(jnp.bfloat16)
    gradient_buffer = populate_slots(queued_rows, expert_batch, param_bundle)
    outs = []
    grads = []
    for expert_unit in range(EXPERTS):
        wg = wg_all[:, expert_unit * HIDDEN_SIZE:(expert_unit + 1) * HIDDEN_SIZE]
        wu = wu_all[:, expert_unit * HIDDEN_SIZE:(expert_unit + 1) * HIDDEN_SIZE]
        down_matrix = wd_all[expert_unit * HIDDEN_SIZE:(expert_unit + 1) * HIDDEN_SIZE, :]
        a = jnp.dot(fbuf[expert_unit], wg, preferred_element_type=jnp.float32)
        b = jnp.dot(fbuf[expert_unit], wu, preferred_element_type=jnp.float32)
        h = (jax.nn.silu(a) * b).astype(jnp.bfloat16)
        hs = h.reshape(-1, GROUP, H_DEV).astype(jnp.float32)
        ws = down_matrix.reshape(GROUP, H_DEV, D).astype(jnp.float32)
        parts = jnp.einsum("rgh,ghd->rgd", hs, ws).astype(jnp.bfloat16)
        outs.append(jnp.sum(parts.astype(jnp.float32), axis=1))
        a2 = jnp.dot(bbuf[expert_unit], wg, preferred_element_type=jnp.float32)
        b2 = jnp.dot(bbuf[expert_unit], wu, preferred_element_type=jnp.float32)
        hidden_grad = jnp.einsum("ou,cu->oc", gradient_buffer[expert_unit].astype(jnp.float32), down_matrix.astype(jnp.float32))
        sg = 1.0 / (1.0 + jnp.exp(-a2))
        da = (hidden_grad * b2 * sg * (1.0 + a2 * (1.0 - sg))).astype(jnp.bfloat16)
        db = (hidden_grad * a2 * sg).astype(jnp.bfloat16)
        das = da.reshape(-1, GROUP, H_DEV).astype(jnp.float32)
        dbs = db.reshape(-1, GROUP, H_DEV).astype(jnp.float32)
        wgs = wg.reshape(D, GROUP, H_DEV).astype(jnp.float32)
        wus = wu.reshape(D, GROUP, H_DEV).astype(jnp.float32)
        back = (jnp.einsum("rgh,dgh->rgd", das, wgs) + jnp.einsum("rgh,dgh->rgd", dbs, wus)).astype(jnp.bfloat16)
        grads.append(jnp.sum(back.astype(jnp.float32), axis=1))
    outs = jnp.stack(outs)
    grads = jnp.stack(grads)
    picked = outs[ef, pf].reshape(TOKENS, TOPK, D)
    y = jnp.sum(norm_f[:, :, None] * picked, axis=1).astype(jnp.bfloat16)
    picked_g = grads[expert_batch, param_bundle].reshape(TOKENS, TOPK, D)
    dx = jnp.sum(picked_g, axis=1).astype(jnp.bfloat16)
    return y, dx


def reference(fwd_tokens, fwd_routes, fwd_scores, bwd_tokens, bwd_routes, bwd_scores, out_grad, gate_weight, up_weight, down_weight):
    ys = []
    dxs = []
    for section in range(SECTIONS):
        y, dx = section_pass(fwd_tokens[section], fwd_routes[section], fwd_scores[section],
                             bwd_tokens[section], bwd_routes[section], bwd_scores[section],
                             out_grad[section], gate_weight[section], up_weight[section], down_weight[section])
        ys.append(y)
        dxs.append(dx)
    ys = jnp.stack(ys)
    dxs = jnp.stack(dxs)
    return jnp.roll(ys, 1, axis=0), jnp.roll(dxs, -1, axis=0)
```

```python
import functools

import jax
import jax.numpy as jnp
from jax import lax
from jax.experimental import pallas as pl
from jax.experimental.pallas import tpu as pltpu
from jax.sharding import PartitionSpec as P

GROUP = 8
CHUNKS = 4
F32 = jnp.float32
BF16 = jnp.bfloat16


def flip(value, mask):
    out, bit = value, 1
    while bit <= mask:
        if mask & bit:
            out = out + bit - 2 * bit * (lax.div(value, bit) % 2)
        bit *= 2
    return out


def nt(a, b):
    return lax.dot_general(a, b, (((1,), (1,)), ((), ())), preferred_element_type=F32)


def nn(a, b):
    return jnp.dot(a, b, preferred_element_type=F32)


def kernel(
    experts, cap, slot, chunks,
    info, info_t, tok_f, tok_b, grad, wg, wu, wd, y_ref, dx_ref,
    bundles, gathered, acc, hidden, away, near, from_pair, summed, diag, relay,
    from_x, from_y, back, home,
    z_s, z_r, own_s, own_r, dia_s, dia_r, pair_s, pair_r,
    op_s, op_r, dg_s, dg_r, x_s, x_r, y_s, y_r, b_s, b_r,
):
    tokens, width = tok_f.shape
    cols = width // chunks
    rows = experts * slot
    live = 2 * cap
    outs = experts * live
    me = lax.axis_index("expert")
    mine = lax.div(me, GROUP)
    pair, chip_x, chip_y = flip(me, 1), flip(me, 2), flip(me, 4)
    planes = [None] + [flip(mine, d) * GROUP + lax.rem(me, GROUP) for d in range(1, experts)]

    def copy(src, dst, send, recv, target):
        return pltpu.make_async_remote_copy(
            src_ref=src, dst_ref=dst, send_sem=send, recv_sem=recv,
            device_id={"expert": target}, device_id_type=pl.DeviceIdType.MESH,
        )

    def z_copy(c, d):
        return copy(bundles.at[c, d], gathered.at[c, 0, d], z_s.at[c, d], z_r.at[c, d], planes[d])

    def own_copy(c, k):
        return copy(gathered.at[c, 0], gathered.at[c, k], own_s.at[c, k], own_r.at[c, k],
                    chip_x if k == 1 else chip_y)

    def dia_copy(c):
        k, target = (1, chip_y) if c % 2 == 0 else (2, chip_x)
        return copy(gathered.at[c, k], gathered.at[c, 3], dia_s.at[c], dia_r.at[c], target)

    def pair_copy(c, k):
        return copy(gathered.at[c, k], gathered.at[c, 4 + k], pair_s.at[c, k], pair_r.at[c, k], pair)

    def op_copy(c):
        return copy(away.at[c], from_pair.at[c], op_s.at[c], op_r.at[c], pair)

    def dg_copy(c):
        return copy(summed.at[c, 3], diag.at[c], dg_s.at[c], dg_r.at[c],
                    chip_x if c % 2 == 0 else chip_y)

    def x_copy(c):
        src = summed.at[c, 1] if c % 2 == 0 else relay.at[c]
        return copy(src, from_x.at[c], x_s.at[c], x_r.at[c], chip_x)

    def y_copy(c):
        src = relay.at[c] if c % 2 == 0 else summed.at[c, 2]
        return copy(src, from_y.at[c], y_s.at[c], y_r.at[c], chip_y)

    def b_copy(c, d):
        return copy(back.at[c, d], home.at[c, d], b_s.at[c, d], b_r.at[c, d], planes[d])

    barrier = pltpu.get_barrier_semaphore()
    friends = [pair, chip_x, chip_y] + planes[1:]
    for friend in friends:
        pl.semaphore_signal(barrier, inc=1, device_id={"expert": friend},
                            device_id_type=pl.DeviceIdType.MESH)

    first = lax.broadcasted_iota(jnp.int32, (tokens, tokens), 0)
    second = lax.broadcasted_iota(jnp.int32, (tokens, tokens), 1)
    up = (first < second).astype(F32)
    low = (second < first).astype(F32)
    place_r = lax.broadcasted_iota(jnp.int32, (rows, tokens), 0).astype(F32)
    place_c = lax.broadcasted_iota(jnp.int32, (tokens, rows), 1).astype(F32)
    pick_f = jnp.zeros((rows, tokens), F32)
    pick_x = jnp.zeros((rows, tokens), F32)
    pick_g = jnp.zeros((rows, tokens), F32)
    gain = jnp.zeros((rows, 1), F32)
    join_f = jnp.zeros((tokens, rows), F32)
    join_b = jnp.zeros((tokens, rows), F32)
    norm_r = info_t[6:7, :] + info_t[7:8, :]
    norm_c = info[:, 4:5] + info[:, 5:6]
    for d in range(experts):
        want = flip(mine, d).astype(F32)
        for b in (0, 2):
            row0, row1 = info_t[b:b + 1, :] == want, info_t[b + 1:b + 2, :] == want
            col0, col1 = info[:, b:b + 1] == want, info[:, b + 1:b + 2] == want
            in_row = row0 | row1
            in_col = col0 | col1
            rank_r = jnp.sum(jnp.where(in_col, up, 0.0), axis=0, keepdims=True)
            rank_c = jnp.sum(jnp.where(in_row, low, 0.0), axis=1, keepdims=True)
            rank_r = jnp.where(in_row, rank_r, -1e6) + float(d * slot)
            rank_c = jnp.where(in_col, rank_c, -1e6) + float(d * slot)
            if b == 0:
                pick_f = pick_f + (place_r == rank_r).astype(F32)
                weight = jnp.where(col0, info[:, 4:5], info[:, 5:6]) / norm_c
                join_f = join_f + jnp.where(place_c == rank_c, weight, 0.0)
            else:
                pick_x = pick_x + (place_r == rank_r + cap).astype(F32)
                hit = place_r == rank_r + 2 * cap
                pick_g = pick_g + hit.astype(F32)
                weight = jnp.where(row0, info_t[6:7, :], info_t[7:8, :]) / norm_r
                gain = gain + jnp.sum(jnp.where(hit, weight, 0.0), axis=1, keepdims=True)
                join_b = join_b + (place_c == rank_c + cap).astype(F32)
    pick_f, pick_x, pick_g = pick_f.astype(BF16), pick_x.astype(BF16), pick_g.astype(BF16)
    high = join_f.astype(BF16)
    rest = join_f - high.astype(F32)
    middle = rest.astype(BF16)
    last = (rest - middle.astype(F32)).astype(BF16)
    join = jnp.concatenate([high, middle, last, join_b.astype(BF16)], axis=0)

    pl.semaphore_wait(barrier, len(friends))
    for c in range(chunks):
        at = slice(c * cols, (c + 1) * cols)
        block = nn(pick_f, tok_f[:, at]) + nn(pick_x, tok_b[:, at]) + gain * nn(pick_g, grad[:, at])
        block = block.astype(BF16).reshape(experts, slot, cols)
        gathered[c, 0, 0] = block[0]
        for d in range(1, experts):
            bundles[c, d] = block[d]
            z_copy(c, d).start()

    acc[...] = jnp.zeros_like(acc)

    def gather_own(c):
        for d in range(1, experts):
            z_copy(c, d).wait_recv()
        own_copy(c, 1).start()
        own_copy(c, 2).start()
        pair_copy(c, 0).start()

    def gather_next(c):
        order = (1, 2) if c % 2 == 0 else (2, 1)
        own_copy(c, order[0]).wait_recv()
        dia_copy(c).start()
        pair_copy(c, order[0]).start()
        own_copy(c, order[1]).wait_recv()
        pair_copy(c, order[1]).start()

    def gather_last(c):
        dia_copy(c).wait_recv()
        pair_copy(c, 3).start()

    def multiply(c):
        for k in range(4):
            pair_copy(c, k).wait_recv()
        at = slice(c * cols, (c + 1) * cols)

        def one(q, carry):
            part = gathered[c, q].reshape(rows, cols)
            acc[q, :, 0:128] += nn(part, wg[at, :])
            acc[q, :, 128:256] += nn(part, wu[at, :])
            acc[q, :, 256:384] += nt(part, wd[:, at])
            return carry

        lax.fori_loop(0, 8, one, 0)

    for step in range(chunks + 3):
        for lag, stage in enumerate((gather_own, gather_next, gather_last, multiply)):
            if 0 <= step - lag < chunks:
                stage(step - lag)

    out_i = lax.broadcasted_iota(jnp.int32, (outs, rows), 0)
    in_i = lax.broadcasted_iota(jnp.int32, (outs, rows), 1)
    squeeze = jnp.zeros((outs, rows), F32)
    out_t = lax.broadcasted_iota(jnp.int32, (rows, outs), 1)
    in_t = lax.broadcasted_iota(jnp.int32, (rows, outs), 0)
    spread = jnp.zeros((rows, outs), F32)
    for d in range(experts):
        shift = d * (slot - live)
        squeeze = squeeze + ((in_i == out_i + shift) & (out_i >= d * live) & (out_i < (d + 1) * live)).astype(F32)
        spread = spread + ((in_t == out_t + shift) & (out_t >= d * live) & (out_t < (d + 1) * live)).astype(F32)
    squeeze, spread = squeeze.astype(BF16), spread.astype(BF16)
    place = lax.broadcasted_iota(jnp.int32, (rows, 128), 0) % slot
    is_f = place < cap
    is_x = (place >= cap) & (place < 2 * cap)

    def activate(q, carry):
        a, b = acc[q, :, 0:128], acc[q, :, 128:256]
        dh = pltpu.roll(acc[q, :, 256:384], rows - cap, 0)
        sg = 1.0 / (1.0 + jnp.exp(-a))
        h = jnp.where(is_f, a * sg * b, 0.0).astype(BF16)
        da = jnp.where(is_x, dh * b * sg * (1.0 + a * (1.0 - sg)), 0.0).astype(BF16)
        db = jnp.where(is_x, dh * a * sg, 0.0).astype(BF16)
        hidden[q, :, 0:128] = nn(squeeze, h).astype(BF16)
        hidden[q, :, 128:256] = nn(squeeze, da).astype(BF16)
        hidden[q, :, 256:384] = nn(squeeze, db).astype(BF16)
        return carry

    lax.fori_loop(0, 8, activate, 0)

    def partial(q, c):
        at = slice(c * cols, (c + 1) * cols)
        total = nn(hidden[q, :, 0:128], wd[:, at])
        total = total + nt(hidden[q, :, 128:256], wg[at, :])
        total = total + nt(hidden[q, :, 256:384], wu[at, :])
        return total.astype(BF16)

    def produce(c):
        def far(r, carry):
            away[c, r] = partial(4 + r, c)
            return carry

        def close(r, carry):
            near[c, r] = partial(r, c)
            return carry

        lax.fori_loop(0, 4, far, 0)
        op_copy(c).start()
        lax.fori_loop(0, 4, close, 0)

    def chip_sum(c):
        op_copy(c).wait_recv()

        def add(r, carry):
            summed[c, r] = (near[c, r].astype(F32) + from_pair[c, r].astype(F32)).astype(BF16)
            return carry

        lax.fori_loop(0, 4, add, 0)
        dg_copy(c).start()
        if c % 2 == 0:
            x_copy(c).start()
        else:
            y_copy(c).start()

    def pass_on(c):
        dg_copy(c).wait_recv()
        k = 2 if c % 2 == 0 else 1
        relay[c] = (summed[c, k].astype(F32) + diag[c].astype(F32)).astype(BF16)
        if c % 2 == 0:
            y_copy(c).start()
        else:
            x_copy(c).start()

    def give_back(c):
        x_copy(c).wait_recv()
        y_copy(c).wait_recv()
        total = summed[c, 0].astype(F32) + from_x[c].astype(F32) + from_y[c].astype(F32)
        wide = nn(spread, total.astype(BF16)).astype(BF16).reshape(experts, slot, cols)
        home[c, 0] = wide[0]
        for d in range(1, experts):
            back[c, d] = wide[d]
            b_copy(c, d).start()

    def finish(c):
        for d in range(1, experts):
            b_copy(c, d).wait_recv()
        at = slice(c * cols, (c + 1) * cols)
        got = nn(join, home[c].reshape(rows, cols))
        t = tokens
        y_ref[:, at] = (got[0:t] + got[t:2 * t] + got[2 * t:3 * t]).astype(BF16)
        dx_ref[:, at] = got[3 * t:4 * t].astype(BF16)

    for step in range(chunks + 4):
        for lag, stage in enumerate((produce, chip_sum, pass_on, give_back, finish)):
            if 0 <= step - lag < chunks:
                stage(step - lag)

    for c in range(chunks):
        for d in range(1, experts):
            z_copy(c, d).wait_send()
            b_copy(c, d).wait_send()
        for k in (1, 2):
            own_copy(c, k).wait_send()
        for k in range(4):
            pair_copy(c, k).wait_send()
        for made in (dia_copy, op_copy, dg_copy, x_copy, y_copy):
            made(c).wait_send()


def body(
    fwd_tokens, fwd_routes, fwd_scores, bwd_tokens, bwd_routes, bwd_scores,
    out_grad, gate_weight, up_weight, down_weight,
):
    experts = lax.axis_size("expert") // GROUP
    tokens, width = fwd_tokens.shape[1:]
    topk = fwd_routes.shape[2]
    cap = min(tokens, max(6, (tokens * topk + experts - 1) // experts + 2))
    slot = -(-3 * cap // 16) * 16
    rows, outs = experts * slot, experts * 2 * cap
    chunks = CHUNKS
    cols = width // chunks
    info = jnp.concatenate(
        [fwd_routes[0].astype(F32), bwd_routes[0].astype(F32), fwd_scores[0], bwd_scores[0]], axis=1
    )
    dma = pltpu.SemaphoreType.DMA
    vmem = lambda *shape: pltpu.VMEM(shape, BF16)
    y, dx = pl.pallas_call(
        functools.partial(kernel, experts, cap, slot, chunks),
        out_shape=[jax.ShapeDtypeStruct((tokens, width), BF16)] * 2,
        in_specs=[pl.BlockSpec(memory_space=pltpu.VMEM)] * 8,
        out_specs=[pl.BlockSpec(memory_space=pltpu.VMEM)] * 2,
        scratch_shapes=[
            vmem(chunks, experts, slot, cols),
            vmem(chunks, 8, experts, slot, cols),
            pltpu.VMEM((8, rows, 384), F32),
            vmem(8, outs, 384),
            vmem(chunks, 4, outs, cols),
            vmem(chunks, 4, outs, cols),
            vmem(chunks, 4, outs, cols),
            vmem(chunks, 4, outs, cols),
            vmem(chunks, outs, cols),
            vmem(chunks, outs, cols),
            vmem(chunks, outs, cols),
            vmem(chunks, outs, cols),
            vmem(chunks, experts, slot, cols),
            vmem(chunks, experts, slot, cols),
            dma((chunks, experts)), dma((chunks, experts)),
            dma((chunks, 3)), dma((chunks, 3)),
            dma((chunks,)), dma((chunks,)),
            dma((chunks, 4)), dma((chunks, 4)),
            dma((chunks,)), dma((chunks,)),
            dma((chunks,)), dma((chunks,)),
            dma((chunks,)), dma((chunks,)),
            dma((chunks,)), dma((chunks,)),
            dma((chunks, experts)), dma((chunks, experts)),
        ],
        compiler_params=pltpu.CompilerParams(
            collective_id=0, has_side_effects=True, vmem_limit_bytes=58 * 1024 * 1024
        ),
    )(info, info.T, fwd_tokens[0], bwd_tokens[0], out_grad[0],
      gate_weight[0], up_weight[0], down_weight[0])
    y, dx = y[None], dx[None]
    count = lax.axis_size("pipe")
    if count > 1:
        y = lax.ppermute(y, "pipe", [(s, (s + 1) % count) for s in range(count)])
        dx = lax.ppermute(dx, "pipe", [(s, (s - 1) % count) for s in range(count)])
    return (y, dx)


def solution(mesh):
    row = P("pipe", "expert", None)
    placed = (row,) * 7 + (P("pipe", None, "expert"), P("pipe", None, "expert"), row)
    return jax.shard_map(
        body, mesh=mesh, in_specs=placed, out_specs=(row, row), check_vma=False
    )
```

```python
import functools

import jax
import jax.numpy as jnp
from jax import lax
from jax.experimental import pallas as pl
from jax.experimental.pallas import tpu as pltpu
from jax.sharding import PartitionSpec as P

GROUP = 8
CHUNKS = 7
F32 = jnp.float32
BF16 = jnp.bfloat16


def flip(value, mask):
    out, bit = value, 1
    while bit <= mask:
        if mask & bit:
            out = out + bit - 2 * bit * (lax.div(value, bit) % 2)
        bit *= 2
    return out


def nt(a, b):
    return lax.dot_general(a, b, (((1,), (1,)), ((), ())), preferred_element_type=F32)


def nn(a, b):
    return jnp.dot(a, b, preferred_element_type=F32)


def kernel(
    experts, cap, slot, chunks,
    info, info_t, tok_f, tok_b, grad, wg, wu, wd, y_ref, dx_ref,
    bundles, gathered, acc, w_in, w_out, hidden, away, near, from_pair, summed, diag, relay,
    from_x, from_y, back, home,
    z_s, z_r, own_s, own_r, dia_s, dia_r, pair_s, pair_r,
    op_s, op_r, dg_s, dg_r, x_s, x_r, y_s, y_r, b_s, b_r,
):
    tokens, width = tok_f.shape
    cols = width // chunks
    rows = experts * slot
    live = 2 * cap
    outs = experts * live
    me = lax.axis_index("expert")
    mine = lax.div(me, GROUP)
    pair, chip_x, chip_y = flip(me, 1), flip(me, 2), flip(me, 4)
    planes = [None] + [flip(mine, d) * GROUP + lax.rem(me, GROUP) for d in range(1, experts)]

    def copy(src, dst, send, recv, target):
        return pltpu.make_async_remote_copy(
            src_ref=src, dst_ref=dst, send_sem=send, recv_sem=recv,
            device_id={"expert": target}, device_id_type=pl.DeviceIdType.MESH,
        )

    def z_copy(c, d):
        return copy(bundles.at[c, d], gathered.at[c, 0, d], z_s.at[c, d], z_r.at[c, d], planes[d])

    def piece(c, k, part):
        return gathered.at[c, k]

    def own_copy(c, p, k):
        return copy(piece(c, 0, p), piece(c, k, p), own_s.at[c, p, k], own_r.at[c, p, k],
                    chip_x if k == 1 else chip_y)

    def dia_copy(c, p):
        k, target = (1, chip_y) if c % 2 == 0 else (2, chip_x)
        return copy(piece(c, k, p), piece(c, 3, p), dia_s.at[c, p], dia_r.at[c, p], target)

    def pair_copy(c, p, k):
        return copy(piece(c, k, p), piece(c, 4 + k, p), pair_s.at[c, p, k], pair_r.at[c, p, k], pair)

    def op_copy(c):
        return copy(away.at[c], from_pair.at[c], op_s.at[c], op_r.at[c], pair)

    def dg_copy(c):
        return copy(summed.at[c, 3], diag.at[c], dg_s.at[c], dg_r.at[c],
                    chip_x if c % 2 == 0 else chip_y)

    def x_copy(c):
        src = summed.at[c, 1] if c % 2 == 0 else relay.at[c]
        return copy(src, from_x.at[c], x_s.at[c], x_r.at[c], chip_x)

    def y_copy(c):
        src = relay.at[c] if c % 2 == 0 else summed.at[c, 2]
        return copy(src, from_y.at[c], y_s.at[c], y_r.at[c], chip_y)

    def b_copy(c, d):
        return copy(back.at[c, d], home.at[c, d], b_s.at[c, d], b_r.at[c, d], planes[d])

    barrier = pltpu.get_barrier_semaphore()
    friends = [pair, chip_x, chip_y] + planes[1:]
    for friend in friends:
        pl.semaphore_signal(barrier, inc=1, device_id={"expert": friend},
                            device_id_type=pl.DeviceIdType.MESH)

    first = lax.broadcasted_iota(jnp.int32, (tokens, tokens), 0)
    second = lax.broadcasted_iota(jnp.int32, (tokens, tokens), 1)
    up = (first < second).astype(F32)
    low = (second < first).astype(F32)
    place_r = lax.broadcasted_iota(jnp.int32, (rows, tokens), 0).astype(F32)
    place_c = lax.broadcasted_iota(jnp.int32, (tokens, rows), 1).astype(F32)
    pick_f = jnp.zeros((rows, tokens), F32)
    pick_x = jnp.zeros((rows, tokens), F32)
    pick_g = jnp.zeros((rows, tokens), F32)
    gain = jnp.zeros((rows, 1), F32)
    join_f = jnp.zeros((tokens, rows), F32)
    join_b = jnp.zeros((tokens, rows), F32)
    norm_r = info_t[6:7, :] + info_t[7:8, :]
    norm_c = info[:, 4:5] + info[:, 5:6]
    for d in range(experts):
        want = flip(mine, d).astype(F32)
        for b in (0, 2):
            row0, row1 = info_t[b:b + 1, :] == want, info_t[b + 1:b + 2, :] == want
            col0, col1 = info[:, b:b + 1] == want, info[:, b + 1:b + 2] == want
            in_row = row0 | row1
            in_col = col0 | col1
            rank_r = jnp.sum(jnp.where(in_col, up, 0.0), axis=0, keepdims=True)
            rank_c = jnp.sum(jnp.where(in_row, low, 0.0), axis=1, keepdims=True)
            rank_r = jnp.where(in_row, rank_r, -1e6) + float(d * slot)
            rank_c = jnp.where(in_col, rank_c, -1e6) + float(d * slot)
            if b == 0:
                pick_f = pick_f + (place_r == rank_r).astype(F32)
                weight = jnp.where(col0, info[:, 4:5], info[:, 5:6]) / norm_c
                join_f = join_f + jnp.where(place_c == rank_c, weight, 0.0)
            else:
                pick_x = pick_x + (place_r == rank_r + cap).astype(F32)
                hit = place_r == rank_r + 2 * cap
                pick_g = pick_g + hit.astype(F32)
                weight = jnp.where(row0, info_t[6:7, :], info_t[7:8, :]) / norm_r
                gain = gain + jnp.sum(jnp.where(hit, weight, 0.0), axis=1, keepdims=True)
                join_b = join_b + (place_c == rank_c + cap).astype(F32)
    pick_f, pick_x, pick_g = pick_f.astype(BF16), pick_x.astype(BF16), pick_g.astype(BF16)
    high = join_f.astype(BF16)
    rest = join_f - high.astype(F32)
    middle = rest.astype(BF16)
    last = (rest - middle.astype(F32)).astype(BF16)
    join = jnp.concatenate([high, middle, last, join_b.astype(BF16)], axis=0)

    def send_own(c, p):
        own_copy(c, p, 1).start()
        own_copy(c, p, 2).start()
        pair_copy(c, p, 0).start()

    pl.semaphore_wait(barrier, len(friends))
    for c in range(chunks):
        at = slice(c * cols, (c + 1) * cols)
        block = nn(pick_f, tok_f[:, at]) + nn(pick_x, tok_b[:, at]) + gain * nn(pick_g, grad[:, at])
        block = block.astype(BF16).reshape(experts, slot, cols)
        for d in range(1, experts):
            bundles[c, d] = block[d]
            z_copy(c, d).start()
        gathered[c, 0, 0] = block[0]

    acc[...] = jnp.zeros_like(acc)

    corner0 = lax.broadcasted_iota(jnp.int32, (128, 128), 0)
    corner1 = lax.broadcasted_iota(jnp.int32, (128, 128), 1)
    eye = (corner0 == corner1).astype(F32).astype(BF16)

    def gather_own(c):
        at = slice(c * cols, (c + 1) * cols)
        w_in[c, :, 0:128] = wg[at, :]
        w_in[c, :, 128:256] = wu[at, :]
        w_out[c, 0:128, :] = wd[:, at]
        w_out[c, 128:256, :] = nt(eye, wg[at, :]).astype(BF16)
        w_out[c, 256:384, :] = nt(eye, wu[at, :]).astype(BF16)
        for d in range(1, experts):
            z_copy(c, d).wait_recv()
        send_own(c, 1)

    def gather_next(c, p):
        order = (1, 2) if c % 2 == 0 else (2, 1)
        own_copy(c, p, order[0]).wait_recv()
        dia_copy(c, p).start()
        pair_copy(c, p, order[0]).start()
        own_copy(c, p, order[1]).wait_recv()
        pair_copy(c, p, order[1]).start()

    def gather_last(c, p):
        dia_copy(c, p).wait_recv()
        pair_copy(c, p, 3).start()

    def multiply(c):
        for p in (1,):
            for k in range(4):
                pair_copy(c, p, k).wait_recv()
        at = slice(c * cols, (c + 1) * cols)

        def one(h, carry):
            half = pl.ds(4 * h, 4)
            part = gathered[c, half].reshape(4 * rows, cols)
            acc[half, :, 0:256] += nn(part, w_in[c]).reshape(4, rows, 256)
            acc[half, :, 256:384] += nt(part, wd[:, at]).reshape(4, rows, 128)
            return carry

        lax.fori_loop(0, 2, one, 0)

    for step in range(chunks + 3):
        if step < chunks:
            gather_own(step)
        if 0 <= step - 1 < chunks:
            gather_next(step - 1, 1)
        if 0 <= step - 2 < chunks:
            gather_last(step - 2, 1)
        if 0 <= step - 3:
            multiply(step - 3)

    out_i = lax.broadcasted_iota(jnp.int32, (outs, rows), 0)
    in_i = lax.broadcasted_iota(jnp.int32, (outs, rows), 1)
    squeeze = jnp.zeros((outs, rows), F32)
    out_t = lax.broadcasted_iota(jnp.int32, (rows, outs), 1)
    in_t = lax.broadcasted_iota(jnp.int32, (rows, outs), 0)
    spread = jnp.zeros((rows, outs), F32)
    for d in range(experts):
        shift = d * (slot - live)
        squeeze = squeeze + ((in_i == out_i + shift) & (out_i >= d * live) & (out_i < (d + 1) * live)).astype(F32)
        spread = spread + ((in_t == out_t + shift) & (out_t >= d * live) & (out_t < (d + 1) * live)).astype(F32)
    squeeze, spread = squeeze.astype(BF16), spread.astype(BF16)
    place = lax.broadcasted_iota(jnp.int32, (rows, 128), 0) % slot
    is_f = place < cap
    is_x = (place >= cap) & (place < 2 * cap)

    def activate(q, carry):
        a, b = acc[q, :, 0:128], acc[q, :, 128:256]
        dh = pltpu.roll(acc[q, :, 256:384], rows - cap, 0)
        sg = 1.0 / (1.0 + jnp.exp(-a))
        h = jnp.where(is_f, a * sg * b, 0.0).astype(BF16)
        da = jnp.where(is_x, dh * b * sg * (1.0 + a * (1.0 - sg)), 0.0).astype(BF16)
        db = jnp.where(is_x, dh * a * sg, 0.0).astype(BF16)
        hidden[q, :, 0:128] = nn(squeeze, h).astype(BF16)
        hidden[q, :, 128:256] = nn(squeeze, da).astype(BF16)
        hidden[q, :, 256:384] = nn(squeeze, db).astype(BF16)
        return carry

    lax.fori_loop(0, 8, activate, 0)

    def partial(q, c):
        total = nn(hidden[q:q + 4].reshape(4 * outs, 384), w_out[c])
        return total.astype(BF16).reshape(4, outs, cols)

    def produce(c):
        away[c] = partial(4, c)
        op_copy(c).start()
        near[c] = partial(0, c)

    def chip_sum(c):
        op_copy(c).wait_recv()

        def add(r, carry):
            summed[c, r] = (near[c, r].astype(F32) + from_pair[c, r].astype(F32)).astype(BF16)
            return carry

        lax.fori_loop(0, 4, add, 0)
        dg_copy(c).start()
        if c % 2 == 0:
            x_copy(c).start()
        else:
            y_copy(c).start()

    def pass_on(c):
        dg_copy(c).wait_recv()
        k = 2 if c % 2 == 0 else 1
        relay[c] = (summed[c, k].astype(F32) + diag[c].astype(F32)).astype(BF16)
        if c % 2 == 0:
            y_copy(c).start()
        else:
            x_copy(c).start()

    def give_back(c):
        x_copy(c).wait_recv()
        y_copy(c).wait_recv()
        total = summed[c, 0].astype(F32) + from_x[c].astype(F32) + from_y[c].astype(F32)
        wide = nn(spread, total.astype(BF16)).astype(BF16).reshape(experts, slot, cols)
        home[c, 0] = wide[0]
        for d in range(1, experts):
            back[c, d] = wide[d]
            b_copy(c, d).start()

    def finish(c):
        for d in range(1, experts):
            b_copy(c, d).wait_recv()
        at = slice(c * cols, (c + 1) * cols)
        got = nn(join, home[c].reshape(rows, cols))
        t = tokens
        y_ref[:, at] = (got[0:t] + got[t:2 * t] + got[2 * t:3 * t]).astype(BF16)
        dx_ref[:, at] = got[3 * t:4 * t].astype(BF16)

    for step in range(chunks + 4):
        for lag, stage in enumerate((produce, chip_sum, pass_on, give_back, finish)):
            if 0 <= step - lag < chunks:
                stage(step - lag)

    for c in range(chunks):
        for d in range(1, experts):
            z_copy(c, d).wait_send()
            b_copy(c, d).wait_send()
        for p in (1,):
            for k in (1, 2):
                own_copy(c, p, k).wait_send()
            for k in range(4):
                pair_copy(c, p, k).wait_send()
            dia_copy(c, p).wait_send()
        for made in (op_copy, dg_copy, x_copy, y_copy):
            made(c).wait_send()


def body(
    fwd_tokens, fwd_routes, fwd_scores, bwd_tokens, bwd_routes, bwd_scores,
    out_grad, gate_weight, up_weight, down_weight,
):
    experts = lax.axis_size("expert") // GROUP
    tokens, width = fwd_tokens.shape[1:]
    topk = fwd_routes.shape[2]
    cap = min(tokens, max(6, (tokens * topk + experts - 1) // experts + 2))
    slot = -(-3 * cap // 16) * 16
    rows, outs = experts * slot, experts * 2 * cap
    chunks = CHUNKS
    cols = width // chunks
    info = jnp.concatenate(
        [fwd_routes[0].astype(F32), bwd_routes[0].astype(F32), fwd_scores[0], bwd_scores[0]], axis=1
    )
    dma = pltpu.SemaphoreType.DMA
    vmem = lambda *shape: pltpu.VMEM(shape, BF16)
    y, dx = pl.pallas_call(
        functools.partial(kernel, experts, cap, slot, chunks),
        out_shape=[jax.ShapeDtypeStruct((tokens, width), BF16)] * 2,
        in_specs=[pl.BlockSpec(memory_space=pltpu.VMEM)] * 8,
        out_specs=[pl.BlockSpec(memory_space=pltpu.VMEM)] * 2,
        scratch_shapes=[
            vmem(chunks, experts, slot, cols),
            vmem(chunks, 8, experts, slot, cols),
            pltpu.VMEM((8, rows, 384), F32),
            vmem(chunks, cols, 256),
            vmem(chunks, 384, cols),
            vmem(8, outs, 384),
            vmem(chunks, 4, outs, cols),
            vmem(chunks, 4, outs, cols),
            vmem(chunks, 4, outs, cols),
            vmem(chunks, 4, outs, cols),
            vmem(chunks, outs, cols),
            vmem(chunks, outs, cols),
            vmem(chunks, outs, cols),
            vmem(chunks, outs, cols),
            vmem(chunks, experts, slot, cols),
            vmem(chunks, experts, slot, cols),
            dma((chunks, experts)), dma((chunks, experts)),
            dma((chunks, 2, 3)), dma((chunks, 2, 3)),
            dma((chunks, 2)), dma((chunks, 2)),
            dma((chunks, 2, 4)), dma((chunks, 2, 4)),
            dma((chunks,)), dma((chunks,)),
            dma((chunks,)), dma((chunks,)),
            dma((chunks,)), dma((chunks,)),
            dma((chunks,)), dma((chunks,)),
            dma((chunks, experts)), dma((chunks, experts)),
        ],
        compiler_params=pltpu.CompilerParams(
            collective_id=0, has_side_effects=True, vmem_limit_bytes=58 * 1024 * 1024
        ),
    )(info, info.T, fwd_tokens[0], bwd_tokens[0], out_grad[0],
      gate_weight[0], up_weight[0], down_weight[0])
    y, dx = y[None], dx[None]
    count = lax.axis_size("pipe")
    if count > 1:
        y = lax.ppermute(y, "pipe", [(s, (s + 1) % count) for s in range(count)])
        dx = lax.ppermute(dx, "pipe", [(s, (s - 1) % count) for s in range(count)])
    return (y, dx)


def solution(mesh):
    row = P("pipe", "expert", None)
    placed = (row,) * 7 + (P("pipe", None, "expert"), P("pipe", None, "expert"), row)
    return jax.shard_map(
        body, mesh=mesh, in_specs=placed, out_specs=(row, row), check_vma=False
    )
```
